256 devices in a mesh: src: 32 (over x, y, core), tgt: 8 (over z).
Axes of the slice: x: 4, y: 4, z: 8, core: 2. Of those that a mesh axis runs over, the one named last changes fastest.
Arguments:
- sources: float32 [32768, 128], P(('src', 'tgt')), may hold values from -3 to 3
- targets: float32 [32768, 128], P(('tgt', 'src')), may hold values from -0.6 to 0.6
- log_src_mass: float32 [32768], P('src'), may hold values from -1 to 1
- log_tgt_mass: float32 [32768], P('tgt'), may hold values from -1 to 1
Outputs:
- src_potential: float32 [32768], P('src')
- tgt_potential: float32 [32768], P('tgt')
The draws below stay inside these ranges and needn't reach their ends.
All inputs are finite; a program needn't handle non-finite values.
Results may differ from the reference program's by a relative error of at most 0.0003.
Values sent between devices are 32-bit elements; how exact they have to be, the bound alone decides.
No kernel may reach another device: no remote copies, remote signals or barrier semaphores. Data moves between devices by JAX's collectives and lax.ppermute only.
A program may use at most 64 MiB of HBM per device.

```python
import jax
import jax.numpy as jnp
from jax import lax

LATENT = 128
ITERS = 3
NS = 32768
NT = 32768


def draw_sources(key, part):
    key = jax.random.fold_in(key, 1)
    base_key = jax.random.fold_in(key, 0)
    base = jnp.clip(jax.random.normal(base_key, (NS, LATENT), jnp.float32) * 0.09, -0.6, 0.6)
    return base


def levels(stream_key, shape, cuts, smallest, largest):
    level, own = 1.0, jax.random.fold_in(stream_key, 6)
    for position, shards_of in cuts:
        heights = jnp.exp(jax.random.uniform(jax.random.fold_in(own, position), (shards_of,), jnp.float32, smallest / len(cuts), largest / len(cuts)))
        level = level * jnp.repeat(heights, shape[position] // shards_of).reshape([-1 if axis == position else 1 for axis in range(len(shape))])
    return level


def normal_values(stream_key, dims, width, limit, cuts=(), dtype=jnp.bfloat16):
    values = width * jax.random.normal(stream_key, dims, jnp.float32)
    if cuts:
        values = values * levels(stream_key, dims, cuts, -0.22, 0.18)
    return jnp.clip(values, -limit, limit).astype(dtype)


def setup_inputs(seed: int = 0) -> dict:
    splits = jax.random.split(jax.random.key(seed), 5)
    return {
        "sources": draw_sources(jax.random.fold_in(splits[4], 71), 0),
        "targets": normal_values(splits[1], (NT, LATENT), 0.09, 0.6, ((0, 256),), jnp.float32),
        "log_src_mass": jnp.clip(jax.random.uniform(splits[2], (NS,), jnp.float32, -1.0, 1.0) * levels(splits[2], (NS,), ((0, 32),), -0.4, 0.0), -1.0, 1.0),
        "log_tgt_mass": jnp.clip(jax.random.uniform(splits[3], (NT,), jnp.float32, -1.0, 1.0) * levels(splits[3], (NT,), ((0, 8),), -0.4, 0.0), -1.0, 1.0),
    }


eps = 0.05


def cost_block(block, targets, tgt_sq):
    src_sq = jnp.sum(block * block, axis=1)
    cross = jnp.dot(block, targets.T, precision=lax.Precision.HIGHEST, preferred_element_type=jnp.float32)
    return src_sq[:, None] + tgt_sq[None, :] - 2.0 * cross


def reference(sources, targets, log_src_mass, log_tgt_mass):
    blk = min(512, NS)
    count = NS // blk
    src_blocks = sources.reshape(count, blk, LATENT)
    mass_blocks = log_src_mass.reshape(count, blk)
    tgt_sq = jnp.sum(targets * targets, axis=1)
    tgt_potential = jnp.zeros((NT,), jnp.float32)
    src_potential = jnp.zeros((NS,), jnp.float32)
    for step in range(ITERS):
        def row_update(block):
            cost = cost_block(block, targets, tgt_sq)
            expo = log_tgt_mass[None, :] + (tgt_potential[None, :] - cost) / eps
            peak = jnp.max(expo, axis=1)
            total = jnp.sum(jnp.exp(expo - peak[:, None]), axis=1)
            return -eps * (peak + jnp.log(total))

        src_potential = lax.map(row_update, src_blocks).reshape(NS)
        pot_blocks = src_potential.reshape(count, blk)

        def col_update(carry, items):
            peak, total = carry
            block, mass, pot = items
            cost = cost_block(block, targets, tgt_sq)
            expo = mass[:, None] + (pot[:, None] - cost) / eps
            fresh = jnp.maximum(peak, jnp.max(expo, axis=0))
            total = total * jnp.exp(peak - fresh) + jnp.sum(jnp.exp(expo - fresh[None, :]), axis=0)
            return (fresh, total), None

        start = (jnp.full((NT,), -1e30, jnp.float32), jnp.zeros((NT,), jnp.float32))
        (peak, total), unused = lax.scan(col_update, start, (src_blocks, mass_blocks, pot_blocks))
        tgt_potential = -eps * (peak + jnp.log(total))
    return src_potential, tgt_potential
```

```python
import functools

import jax
import jax.numpy as jnp
from jax import lax
from jax.experimental import pallas as pl
from jax.experimental.pallas import tpu as pltpu
from jax.sharding import Mesh
from jax.sharding import PartitionSpec as P

eps = 0.05
KAPPA = 1.0 / eps
SHIFT = 44.0
L = 128
B = 16
N = B * L
F32 = jnp.float32
BF16 = jnp.bfloat16
VM = pl.BlockSpec(memory_space=pltpu.VMEM)


def rows_of(q):
    return pl.ds(pl.multiple_of(q * L, L), L)


def lanes_of(s):
    return pl.ds(s * L, L)


def fold(x, op):
    return op(x.reshape(L // 8, 8, L), axis=0)


def spread(vec, out_ref):
    turned = jnp.concatenate([vec, jnp.zeros((L - B, L), F32)], axis=0).T
    for q in range(B):
        out_ref[q * L : (q + 1) * L, :] = jnp.broadcast_to(turned[:, q : q + 1], (L, L))


def split3(x):
    a = x.astype(BF16)
    x = x - a.astype(F32)
    b = x.astype(BF16)
    x = x - b.astype(F32)
    return a, b, x.astype(BF16)


def start_kernel(src_ref, tgt_ref, lt_ref, ls_ref, z_ref, pay_ref, sq_ref, s6, t6, beta):
    def prepare(q, _):
        rows = rows_of(q)
        s = src_ref[rows, :]
        t = tgt_ref[rows, :]
        sq_ref[pl.ds(q, 1), :] = jnp.sum((s * s).T, axis=0, keepdims=True)
        tsq = jnp.sum((t * t).T, axis=0, keepdims=True)
        beta[pl.ds(q, 1), :] = lt_ref[pl.ds(q, 1), :] - KAPPA * tsq
        s1, s2, s3 = split3(s * (2.0 * KAPPA))
        t1, t2, t3 = split3(t)
        for c, (a, b) in enumerate(((s1, t1), (s1, t2), (s2, t1), (s2, t2), (s1, t3), (s3, t1))):
            s6[rows, c * L : (c + 1) * L] = a
            t6[rows, c * L : (c + 1) * L] = b
        return 0

    lax.fori_loop(0, B, prepare, 0)

    def product(q):
        g = lax.dot_general(s6[rows_of(q), :], t6[...], (((1,), (1,)), ((), ())), preferred_element_type=F32)
        for s in range(B):
            z_ref[rows_of(q), lanes_of(s)] = g[:, s * L : (s + 1) * L] + beta[s : s + 1, :]

    def stats(q):
        rows = rows_of(q)
        peak = z_ref[rows, lanes_of(0)]
        for s in range(1, B):
            peak = jnp.maximum(peak, z_ref[rows, lanes_of(s)])
        total = jnp.zeros((L, L), F32)
        for s in range(B):
            total = total + jnp.exp(z_ref[rows, lanes_of(s)] - peak)
        peak_t = peak.T
        top = jnp.max(peak_t, axis=0, keepdims=True)
        pay_ref[pl.ds(q, 1), :] = top
        pay_ref[pl.ds(B + q, 1), :] = jnp.sum(total.T * jnp.exp(peak_t - top), axis=0, keepdims=True)

    product(0)

    def body(q, _):
        stats(q - 1)
        product(q)
        return 0

    lax.fori_loop(1, B, body, 0)
    stats(B - 1)
    pay_ref[2 * B :, :] = ls_ref[...]


def merge(got_ref):
    peaks = [got_ref[d, :B, :] for d in range(B)]
    top = functools.reduce(jnp.maximum, peaks)
    total = functools.reduce(jnp.add, [got_ref[d, B : 2 * B, :] * jnp.exp(peaks[d] - top) for d in range(B)])
    return top + jnp.log(total)


def add_up(got_ref):
    return functools.reduce(jnp.add, [got_ref[d] for d in range(B)])


def cols_kernel(z_ref, got_ref, pay_ref, alpha_ref, ls_ref, wide):
    ls = jnp.concatenate([got_ref[0, 2 * B :, :], got_ref[B // 2, 2 * B :, :]], axis=0)
    alpha = ls - merge(got_ref)
    alpha_ref[...] = alpha
    ls_ref[...] = ls
    spread(alpha, wide)

    def body(q, carry):
        rows = rows_of(q)
        a = wide[rows, :]
        out = []
        for s in range(B):
            peak, total = carry[s]
            w = z_ref[rows, lanes_of(s)] + a
            fresh = jnp.maximum(peak, fold(w, jnp.max))
            e = jnp.exp(w.reshape(L // 8, 8, L) - fresh[None])
            out.append((fresh, total * jnp.exp(peak - fresh) + jnp.sum(e, axis=0)))
        return tuple(out)

    first = tuple((jnp.full((8, L), -1e30, F32), jnp.zeros((8, L), F32)) for _ in range(B))
    done = lax.fori_loop(0, B, body, first)
    for s in range(B):
        peak, total = done[s]
        top = jnp.max(peak, axis=0, keepdims=True)
        pay_ref[s : s + 1, :] = top
        pay_ref[B + s : B + s + 1, :] = jnp.sum(total * jnp.exp(peak - top), axis=0, keepdims=True)


def exp_kernel(z_ref, got_ref, alpha_ref, lt_ref, k_ref, pay_ref, n_ref, wide, shift):
    n = merge(got_ref)
    n_ref[...] = n
    shift[...] = lt_ref[...] - n + SHIFT
    spread(alpha_ref[...], wide)

    def body(q, _):
        rows = rows_of(q)
        a = wide[rows, :]
        total = jnp.zeros((L, L), F32)
        for s in range(B):
            k = jnp.exp((z_ref[rows, lanes_of(s)] + a) + shift[s : s + 1, :])
            k_ref[rows, lanes_of(s)] = k
            total = total + k
        pay_ref[pl.ds(q, 1), :] = jnp.sum(total.T, axis=0, keepdims=True)
        return 0

    lax.fori_loop(0, B, body, 0)


def col_sums(k_ref, pay_ref, wide):
    def body(q, carry):
        rows = rows_of(q)
        u = wide[rows, :]
        return tuple(carry[s] + fold(k_ref[rows, lanes_of(s)] * u, jnp.sum) for s in range(B))

    done = lax.fori_loop(0, B, body, tuple(jnp.zeros((8, L), F32) for _ in range(B)))
    for s in range(B):
        pay_ref[s : s + 1, :] = jnp.sum(done[s], axis=0, keepdims=True)


def col_kernel(k_ref, got_ref, ls_ref, pay_ref, wide):
    spread(jnp.exp(ls_ref[...]) / add_up(got_ref), wide)
    col_sums(k_ref, pay_ref, wide)


def row_kernel(k_ref, got_ref, lt_ref, pay_ref, scale):
    scale[...] = jnp.exp(lt_ref[...]) / add_up(got_ref)

    def body(q, _):
        rows = rows_of(q)
        total = jnp.zeros((L, L), F32)
        for s in range(B):
            total = total + k_ref[rows, lanes_of(s)] * scale[s : s + 1, :]
        pay_ref[pl.ds(q, 1), :] = jnp.sum(total.T, axis=0, keepdims=True)
        return 0

    lax.fori_loop(0, B, body, 0)


def last_kernel(k_ref, got_ref, ls_ref, alpha_ref, sq_ref, pay_ref, f_ref, wide):
    total = add_up(got_ref)
    f_ref[...] = sq_ref[...] - eps * (jnp.log(total) - SHIFT - alpha_ref[...])
    spread(jnp.exp(ls_ref[...]) / total, wide)
    col_sums(k_ref, pay_ref, wide)


def call(kernel, outs, *args, scratch=(), limit=24, aliases=None, name=None):
    return pl.pallas_call(
        kernel,
        out_shape=[pltpu.VMEM(shape, F32) for shape in outs],
        in_specs=[VM] * len(args),
        out_specs=[VM] * len(outs),
        scratch_shapes=scratch,
        input_output_aliases=aliases or {},
        compiler_params=pltpu.CompilerParams(vmem_limit_bytes=limit * 2**20),
        name=name,
    )(*args)


def share(x, axes):
    return lax.all_to_all(jnp.broadcast_to(x[None], (B,) + x.shape), axes, 0, 0, tiled=True)


ROW = ("c", "z")
COL = ("x", "y")


def local(sources, targets, log_src_mass, log_tgt_mass):
    core = lax.axis_index("c")
    ls_own = log_src_mass.reshape(B // 2, L)
    lt = lax.dynamic_index_in_dim(log_tgt_mass.reshape(B, 2, L), core, 1, keepdims=False)
    src = share(sources, ROW).reshape(N, L)
    tgt = share(targets, COL).reshape(N, L)
    vec, pair, wide = (B, L), (2 * B, L), pltpu.VMEM((N, L), F32)
    bits = [pltpu.VMEM((N, 6 * L), BF16)] * 2 + [pltpu.VMEM(vec, F32)]
    z, pay, sq = call(start_kernel, [(N, N), (2 * B + B // 2, L), vec], src, tgt, lt, ls_own, scratch=bits, name="start")
    pay, alpha, ls = call(cols_kernel, [pair, vec, vec], z, share(pay, ROW), scratch=[wide], name="cols")
    k, pay, n = call(
        exp_kernel, [(N, N), vec, vec], z, share(pay, COL), alpha, lt,
        scratch=[wide, pltpu.VMEM(vec, F32)], aliases={0: 0}, name="exps",
    )
    (pay,) = call(col_kernel, [vec], k, share(pay, ROW), ls, scratch=[wide], name="col")
    (pay,) = call(row_kernel, [vec], k, share(pay, COL), lt, scratch=[pltpu.VMEM(vec, F32)], name="row")
    pay, f = call(last_kernel, [vec, vec], k, share(pay, ROW), ls, alpha, sq, scratch=[wide], name="last")
    total = jnp.sum(share(pay, COL), axis=0)
    g = -eps * (jnp.log(total) + n - 2.0 * lt)
    g = lax.all_gather(g, "c").transpose(1, 0, 2).reshape(2 * N)
    f = lax.dynamic_slice_in_dim(f, core * (B // 2), B // 2, 0).reshape(N // 2)
    return f, g


def solution(mesh):
    grid = Mesh(mesh.devices.reshape(4, 4, 2, 8), ("x", "y", "c", "z"))
    src, tgt = ("x", "y", "c"), "z"
    in_specs = (P((*src, tgt), None), P((tgt, *src), None), P(src), P(tgt))
    return jax.shard_map(local, mesh=grid, in_specs=in_specs, out_specs=(P(src), P(tgt)), check_vma=False)
```

```python
import functools
import math

import jax
import jax.numpy as jnp
from jax import lax
from jax.experimental import pallas as pl
from jax.experimental.pallas import tpu as pltpu
from jax.sharding import Mesh
from jax.sharding import PartitionSpec as P

eps = 0.05
LOG2E = math.log2(math.e)
KAPPA = LOG2E / eps
SHIFT = 43.0
L = 128
B = 16
H = B // 2
N = B * L
F32 = jnp.float32
BF16 = jnp.bfloat16
VM = pl.BlockSpec(memory_space=pltpu.VMEM)
SM = pl.BlockSpec(memory_space=pltpu.SMEM)
VEC = (B, L)
PARTS = ((0, 0), (0, 1), (1, 0), (1, 1), (0, 2), (2, 0))


def rows_of(q):
    return pl.ds(pl.multiple_of(q * L, L), L)


def lanes_of(s):
    return pl.ds(s * L, L)


def fold(x, op):
    return op(x.reshape(-1, 8, L), axis=0)


def spread(vec, out_ref):
    turned = jnp.concatenate([vec, jnp.zeros((L - B, L), F32)], axis=0).T
    for q in range(B):
        out_ref[q * L : (q + 1) * L, :] = jnp.broadcast_to(turned[:, q : q + 1], (L, L))


def split3(x):
    a = x.astype(BF16)
    x = x - a.astype(F32)
    b = x.astype(BF16)
    x = x - b.astype(F32)
    return a, b, x.astype(BF16)


def start_kernel(
    core_ref, own_ref, other_ref, tgt_ref, lt_ref, ls_own_ref, ls_other_ref, z_ref, pay_ref, ls_ref, s6, t6, beta
):
    core = core_ref[0]
    ls_ref[pl.ds(pl.multiple_of(core * H, H), H), :] = ls_own_ref[...]
    ls_ref[pl.ds(pl.multiple_of((1 - core) * H, H), H), :] = ls_other_ref[...]
    for half, ref in ((core, own_ref), (1 - core, other_ref)):
        for q in range(H):
            parts = split3(ref[q * L : (q + 1) * L, :] * (2.0 * KAPPA))
            for c, (a, _) in enumerate(PARTS):
                s6[rows_of(half * H + q), c * L : (c + 1) * L] = parts[a]
    for q in range(B):
        t = tgt_ref[q * L : (q + 1) * L, :].T
        beta[q : q + 1, :] = LOG2E * lt_ref[q : q + 1, :] - KAPPA * jnp.sum(t * t, axis=0, keepdims=True)
        parts = split3(t)
        for c, (_, b) in enumerate(PARTS):
            t6[c * L : (c + 1) * L, q * L : (q + 1) * L] = parts[b]

    for c in range(0, B, 2):
        g = jnp.dot(s6[...], t6[:, c * L : (c + 2) * L], preferred_element_type=F32)
        for s in range(2):
            z_ref[:, lanes_of(c + s)] = g[:, s * L : (s + 1) * L] + beta[c + s : c + s + 1, :]

    def stats(q, _):
        rows = rows_of(q)
        peak = z_ref[rows, lanes_of(0)]
        for s in range(1, B):
            peak = jnp.maximum(peak, z_ref[rows, lanes_of(s)])
        total = jnp.zeros((L, L), F32)
        for s in range(B):
            total = total + jnp.exp2(z_ref[rows, lanes_of(s)] - peak)
        peak = peak.T
        top = jnp.max(peak, axis=0, keepdims=True)
        pay_ref[pl.ds(q, 1), :] = top + jnp.log2(jnp.sum(total.T * jnp.exp2(peak - top), axis=0, keepdims=True))
        return 0

    lax.fori_loop(0, B, stats, 0, unroll=4)


def merge(got_ref):
    got = [got_ref[d] for d in range(B)]
    top = functools.reduce(jnp.maximum, got)
    return top + jnp.log2(functools.reduce(jnp.add, [jnp.exp2(x - top) for x in got]))


def add_up(got_ref):
    return functools.reduce(jnp.add, [got_ref[d] for d in range(B)])


def cols_kernel(z_ref, got_ref, ls_ref, e_ref, pay_ref, m_ref, alpha_ref, wide):
    alpha = LOG2E * ls_ref[...] - merge(got_ref)
    alpha_ref[...] = alpha
    spread(alpha, wide)

    def highest(q, peak):
        a = wide[rows_of(q), :]
        return tuple(jnp.maximum(peak[s], fold(z_ref[rows_of(q), lanes_of(s)] + a, jnp.max)) for s in range(B))

    peak = lax.fori_loop(0, B, highest, (jnp.full((8, L), -1e30, F32),) * B, unroll=2)
    for s in range(B):
        m_ref[s : s + 1, :] = jnp.max(peak[s], axis=0, keepdims=True)

    ahead = 3
    for c in range(0, B, H):

        def weigh(q, total, c=c):
            rows = pl.ds(pl.multiple_of(q * (L // 2), L // 2), L // 2)
            a = wide[rows, :] + SHIFT
            held = [z_ref[rows, lanes_of(c + s)] for s in range(ahead)]
            out = []
            for s in range(H):
                if s + ahead < H:
                    held.append(z_ref[rows, lanes_of(c + s + ahead)])
                e = jnp.exp2((held[s] + a) - m_ref[c + s : c + s + 1, :])
                e_ref[rows, lanes_of(c + s)] = e
                out.append(total[s] + fold(e, jnp.sum))
            return tuple(out)

        total = lax.fori_loop(0, 2 * B, weigh, (jnp.zeros((8, L), F32),) * H, unroll=2)
        for s in range(H):
            one = slice(c + s, c + s + 1)
            pay_ref[one, :] = m_ref[one, :] + (jnp.log2(jnp.sum(total[s], axis=0, keepdims=True)) - SHIFT)


def row_sums(e_ref, v_ref, pay_ref):
    def body(q, _):
        total = jnp.zeros((L, L), F32)
        for s in range(B):
            total = total + e_ref[rows_of(q), lanes_of(s)] * v_ref[s : s + 1, :]
        pay_ref[pl.ds(q, 1), :] = jnp.sum(total.T, axis=0, keepdims=True)
        return 0

    lax.fori_loop(0, B, body, 0, unroll=8)


def col_sums(e_ref, v0_ref, pay_ref, wide):
    def body(q, carry):
        u = wide[rows_of(q), :]
        return tuple(carry[s] + fold(e_ref[rows_of(q), lanes_of(s)] * u, jnp.sum) for s in range(B))

    done = lax.fori_loop(0, B, body, (jnp.zeros((8, L), F32),) * B, unroll=8)
    for s in range(B):
        pay_ref[s : s + 1, :] = v0_ref[s : s + 1, :] * jnp.sum(done[s], axis=0, keepdims=True)


def first_row_kernel(e_ref, got_ref, m_ref, lt_ref, pay_ref, n_ref, v0_ref):
    n = merge(got_ref)
    n_ref[...] = n
    v0_ref[...] = jnp.exp2(m_ref[...] - n + (LOG2E * lt_ref[...] + SHIFT))
    row_sums(e_ref, v0_ref, pay_ref)


def col_kernel(e_ref, got_ref, ls_ref, v0_ref, pay_ref, wide):
    spread(jnp.exp2(LOG2E * ls_ref[...]) / add_up(got_ref), wide)
    col_sums(e_ref, v0_ref, pay_ref, wide)


def row_kernel(e_ref, got_ref, lt_ref, v0_ref, pay_ref, v):
    v[...] = v0_ref[...] * (jnp.exp2(LOG2E * lt_ref[...]) / add_up(got_ref))
    row_sums(e_ref, v, pay_ref)


def last_kernel(core_ref, e_ref, got_ref, ls_ref, v0_ref, alpha_ref, sq_ref, pay_ref, f_ref, wide, total):
    total[...] = add_up(got_ref)
    own = pl.ds(pl.multiple_of(core_ref[0] * H, H), H)
    f_ref[...] = sq_ref[...] - (eps / LOG2E) * (jnp.log2(total[own, :]) - 2.0 * SHIFT - alpha_ref[own, :])
    spread(jnp.exp2(LOG2E * ls_ref[...]) / total[...], wide)
    col_sums(e_ref, v0_ref, pay_ref, wide)


def call(kernel, outs, *args, scratch=(), limit=8, aliases=None):
    return pl.pallas_call(
        kernel,
        out_shape=[pltpu.VMEM(shape, F32) for shape in outs],
        in_specs=[SM if x.dtype == jnp.int32 else VM for x in args],
        out_specs=[VM] * len(outs),
        scratch_shapes=scratch,
        input_output_aliases=aliases or {},
        compiler_params=pltpu.CompilerParams(vmem_limit_bytes=limit * 2**20),
        name=kernel.__name__,
    )(*args)


def share(x, axes, count):
    return lax.all_to_all(jnp.broadcast_to(x[None], (count,) + x.shape), axes, 0, 0, tiled=True)


def over_rows(x):
    return share(x, ("c", "z"), B)


def over_cols(x):
    return share(x, ("x", "y"), B)


def swap(x):
    return lax.ppermute(x, "c", [(0, 1), (1, 0)])


def local(sources, targets, log_src_mass, log_tgt_mass):
    c = lax.axis_index("c")
    core = c.reshape(1)
    ls = log_src_mass.reshape(H, L)
    lt = lax.dynamic_index_in_dim(log_tgt_mass.reshape(B, 2, L), c, 1, keepdims=False)
    own = share(sources, "z", H).reshape(N // 2, L)
    own, sq = lax.optimization_barrier((own, jnp.sum(own * own, axis=1).reshape(H, L)))
    tgt = over_cols(targets).reshape(N, L)
    wide = pltpu.VMEM((N, L), F32)
    bits = [pltpu.VMEM((N, 6 * L), BF16), pltpu.VMEM((6 * L, N), BF16), pltpu.VMEM(VEC, F32)]
    z, pay, ls = call(
        start_kernel, [(N, N), VEC, VEC], core, own, swap(own), tgt, lt, ls, swap(ls), scratch=bits, limit=24
    )
    e, pay, m, alpha = call(cols_kernel, [(N, N), VEC, VEC, VEC], z, over_rows(pay), ls, scratch=[wide], aliases={0: 0})
    pay, n, v0 = call(first_row_kernel, [VEC, VEC, VEC], e, over_cols(pay), m, lt)
    (pay,) = call(col_kernel, [VEC], e, over_rows(pay), ls, v0, scratch=[wide])
    (pay,) = call(row_kernel, [VEC], e, over_cols(pay), lt, v0, scratch=[pltpu.VMEM(VEC, F32)])
    pay, f = call(
        last_kernel, [VEC, (H, L)], core, e, over_rows(pay), ls, v0, alpha, sq, scratch=[wide, pltpu.VMEM(VEC, F32)]
    )
    total = jnp.sum(over_cols(pay), axis=0)
    g = -eps * ((jnp.log2(total) + n) / LOG2E - 2.0 * lt)
    g = lax.all_gather(g, "c").transpose(1, 0, 2).reshape(2 * N)
    return f.reshape(N // 2), g


def solution(mesh):
    grid = Mesh(mesh.devices.reshape(4, 4, 2, 8), ("x", "y", "c", "z"))
    src, tgt = ("x", "y", "c"), "z"
    in_specs = (P((*src, tgt), None), P((tgt, *src), None), P(src), P(tgt))
    return jax.shard_map(local, mesh=grid, in_specs=in_specs, out_specs=(P(src), P(tgt)), check_vma=False)
```

```python
import functools
import math

import jax
import jax.numpy as jnp
from jax import lax
from jax.experimental import pallas as pl
from jax.experimental.pallas import tpu as pltpu
from jax.sharding import Mesh
from jax.sharding import PartitionSpec as P

eps = 0.05
LOG2E = math.log2(math.e)
KAPPA = LOG2E / eps
SHIFT = 43.0
L = 128
B = 16
H = B // 2
N = B * L
F32 = jnp.float32
BF16 = jnp.bfloat16
VM = pl.BlockSpec(memory_space=pltpu.VMEM)
SM = pl.BlockSpec(memory_space=pltpu.SMEM)
VEC = (B, L)
SLABS = 2
NEAR = (0, 1, 7)
FAR = (2, 6, 3, 5, 4)
PARTS = ((0, 0), (0, 1), (1, 0), (1, 1), (0, 2), (2, 0))


def rows_of(q):
    return pl.ds(pl.multiple_of(q * L, L), L)


def lanes_of(s):
    return pl.ds(s * L, L)


def fold(x, op):
    return op(x.reshape(-1, 8, L), axis=0)


def spread(vec, out_ref):
    turned = jnp.concatenate([vec, jnp.zeros((L - B, L), F32)], axis=0).T
    for q in range(B):
        out_ref[q * L : (q + 1) * L, :] = jnp.broadcast_to(turned[:, q : q + 1], (L, L))


def split3(x):
    a = x.astype(BF16)
    x = x - a.astype(F32)
    b = x.astype(BF16)
    x = x - b.astype(F32)
    return a, b, x.astype(BF16)


def start_kernel(
    place_ref, near_ref, near_other_ref, far_ref, far_other_ref, tgt_ref, lt_ref, ls_own_ref, ls_other_ref,
    z_ref, pay_ref, sq_ref, ls_ref, s6, t6, beta,
):
    core, level = place_ref[0], place_ref[1]
    ls_ref[pl.ds(pl.multiple_of(core * H, H), H), :] = ls_own_ref[...]
    ls_ref[pl.ds(pl.multiple_of((1 - core) * H, H), H), :] = ls_other_ref[...]
    for own, order, ref in (
        (True, NEAR, near_ref), (False, NEAR, near_other_ref), (True, FAR, far_ref), (False, FAR, far_other_ref),
    ):
        for at, step in enumerate(order):
            x = ref[at * L : (at + 1) * L, :]
            q = lax.rem(level + (H - step), H)
            if own:
                sq_ref[pl.ds(q, 1), :] = jnp.sum((x * x).T, axis=0, keepdims=True)
            parts = split3(x * (2.0 * KAPPA))
            rows = rows_of((core if own else 1 - core) * H + q)
            for c, (a, _) in enumerate(PARTS):
                s6[rows, c * L : (c + 1) * L] = parts[a]
    for q in range(B):
        t = tgt_ref[q * L : (q + 1) * L, :].T
        beta[q : q + 1, :] = LOG2E * lt_ref[q : q + 1, :] - KAPPA * jnp.sum(t * t, axis=0, keepdims=True)
        parts = split3(t)
        for c, (_, b) in enumerate(PARTS):
            t6[c * L : (c + 1) * L, q * L : (q + 1) * L] = parts[b]

    def product(rows, c):
        g = jnp.dot(s6[rows, :], t6[:, c * L : (c + 2) * L], preferred_element_type=F32)
        for s in range(2):
            z_ref[rows, lanes_of(c + s)] = g[:, s * L : (s + 1) * L] + beta[c + s : c + s + 1, :]

    def stats(q):
        rows = pl.ds(q * L, L)
        peak = z_ref[rows, lanes_of(0)]
        for s in range(1, B):
            peak = jnp.maximum(peak, z_ref[rows, lanes_of(s)])
        total = jnp.zeros((L, L), F32)
        for s in range(B):
            total = total + jnp.exp2(z_ref[rows, lanes_of(s)] - peak)
        peak = peak.T
        top = jnp.max(peak, axis=0, keepdims=True)
        pay_ref[q : q + 1, :] = top + jnp.log2(jnp.sum(total.T * jnp.exp2(peak - top), axis=0, keepdims=True))

    tall = B // SLABS
    for slab in range(SLABS + 1):
        for step in range(H):
            if slab < SLABS:
                product(pl.ds(slab * tall * L, tall * L), 2 * step)
            if slab and step % (H // tall) == 0:
                stats((slab - 1) * tall + step // (H // tall))


def merge(got_ref):
    got = [got_ref[d] for d in range(B)]
    top = functools.reduce(jnp.maximum, got)
    return top + jnp.log2(functools.reduce(jnp.add, [jnp.exp2(x - top) for x in got]))


def add_up(got_ref):
    return functools.reduce(jnp.add, [got_ref[d] for d in range(B)])


def cols_kernel(z_ref, got_ref, ls_ref, e_ref, pay_ref, m_ref, alpha_ref, wide):
    alpha = LOG2E * ls_ref[...] - merge(got_ref)
    alpha_ref[...] = alpha
    spread(alpha, wide)

    def highest(q, peak):
        a = wide[rows_of(q), :]
        return tuple(jnp.maximum(peak[s], fold(z_ref[rows_of(q), lanes_of(s)] + a, jnp.max)) for s in range(B))

    peak = lax.fori_loop(0, B, highest, (jnp.full((8, L), -1e30, F32),) * B, unroll=2)
    for s in range(B):
        m_ref[s : s + 1, :] = jnp.max(peak[s], axis=0, keepdims=True)

    ahead = 3
    for c in range(0, B, H):

        def weigh(q, total, c=c):
            rows = pl.ds(pl.multiple_of(q * (L // 2), L // 2), L // 2)
            a = wide[rows, :] + SHIFT
            held = [z_ref[rows, lanes_of(c + s)] for s in range(ahead)]
            out = []
            for s in range(H):
                if s + ahead < H:
                    held.append(z_ref[rows, lanes_of(c + s + ahead)])
                e = jnp.exp2((held[s] + a) - m_ref[c + s : c + s + 1, :])
                e_ref[rows, lanes_of(c + s)] = e
                out.append(total[s] + fold(e, jnp.sum))
            return tuple(out)

        total = lax.fori_loop(0, 2 * B, weigh, (jnp.zeros((8, L), F32),) * H, unroll=2)
        for s in range(H):
            one = slice(c + s, c + s + 1)
            pay_ref[one, :] = m_ref[one, :] + (jnp.log2(jnp.sum(total[s], axis=0, keepdims=True)) - SHIFT)


def row_sums(e_ref, v_ref, pay_ref):
    def body(q, _):
        total = jnp.zeros((L, L), F32)
        for s in range(B):
            total = total + e_ref[rows_of(q), lanes_of(s)] * v_ref[s : s + 1, :]
        pay_ref[pl.ds(q, 1), :] = jnp.sum(total.T, axis=0, keepdims=True)
        return 0

    lax.fori_loop(0, B, body, 0, unroll=8)


def col_sums(e_ref, v0_ref, pay_ref, wide):
    def body(q, carry):
        u = wide[rows_of(q), :]
        return tuple(carry[s] + fold(e_ref[rows_of(q), lanes_of(s)] * u, jnp.sum) for s in range(B))

    done = lax.fori_loop(0, B, body, (jnp.zeros((8, L), F32),) * B, unroll=8)
    for s in range(B):
        pay_ref[s : s + 1, :] = v0_ref[s : s + 1, :] * jnp.sum(done[s], axis=0, keepdims=True)


def first_row_kernel(e_ref, got_ref, m_ref, lt_ref, pay_ref, n_ref, v0_ref):
    n = merge(got_ref)
    n_ref[...] = n
    v0_ref[...] = jnp.exp2(m_ref[...] - n + (LOG2E * lt_ref[...] + SHIFT))
    row_sums(e_ref, v0_ref, pay_ref)


def col_kernel(e_ref, got_ref, ls_ref, v0_ref, pay_ref, wide):
    spread(jnp.exp2(LOG2E * ls_ref[...]) / add_up(got_ref), wide)
    col_sums(e_ref, v0_ref, pay_ref, wide)


def row_kernel(e_ref, got_ref, lt_ref, v0_ref, pay_ref, v):
    v[...] = v0_ref[...] * (jnp.exp2(LOG2E * lt_ref[...]) / add_up(got_ref))
    row_sums(e_ref, v, pay_ref)


def last_kernel(place_ref, e_ref, got_ref, ls_ref, v0_ref, alpha_ref, sq_ref, pay_ref, f_ref, wide, total):
    total[...] = add_up(got_ref)
    own = pl.ds(pl.multiple_of(place_ref[0] * H, H), H)
    f_ref[...] = sq_ref[...] - (eps / LOG2E) * (jnp.log2(total[own, :]) - 2.0 * SHIFT - alpha_ref[own, :])
    spread(jnp.exp2(LOG2E * ls_ref[...]) / total[...], wide)
    col_sums(e_ref, v0_ref, pay_ref, wide)


def call(kernel, outs, *args, scratch=(), limit=8, aliases=None):
    return pl.pallas_call(
        kernel,
        out_shape=[pltpu.VMEM(x, F32) if isinstance(x, tuple) else x for x in outs],
        in_specs=[SM if x.dtype == jnp.int32 else VM for x in args],
        out_specs=[VM] * len(outs),
        scratch_shapes=scratch,
        input_output_aliases=aliases or {},
        compiler_params=pltpu.CompilerParams(vmem_limit_bytes=limit * 2**20),
        name=kernel.__name__,
    )(*args)


def share(x, axes):
    return lax.all_to_all(jnp.broadcast_to(x[None], (B,) + x.shape), axes, 0, 0, tiled=True)


def over_rows(x):
    return share(x, ("c", "z"))


def over_cols(x):
    return share(x, ("x", "y"))


def swap(x):
    return lax.ppermute(x, "c", [(0, 1), (1, 0)])


def climb(x, step):
    return lax.ppermute(x, "z", [(z, (z + step) % H) for z in range(H)])


def local(sources, targets, log_src_mass, log_tgt_mass):
    c = lax.axis_index("c")
    place = jnp.stack([c, lax.axis_index("z")])
    ls = log_src_mass.reshape(H, L)
    lt = lax.dynamic_index_in_dim(log_tgt_mass.reshape(B, 2, L), c, 1, keepdims=False)
    tgt = over_cols(targets).reshape(N, L)
    near = jnp.concatenate([sources] + [climb(sources, step) for step in NEAR[1:]])
    far = jnp.concatenate([climb(sources, step) for step in FAR])
    wide = pltpu.VMEM((N, L), F32)
    bits = [pltpu.VMEM((N, 6 * L), BF16), pltpu.VMEM((6 * L, N), BF16), pltpu.VMEM(VEC, F32)]
    z, pay, sq, ls = call(
        start_kernel, [(N, N), VEC, (H, L), VEC], place, near, swap(near), far, swap(far), tgt, lt, ls, swap(ls),
        scratch=bits, limit=24,
    )
    e, pay, m, alpha = call(cols_kernel, [(N, N), VEC, VEC, VEC], z, over_rows(pay), ls, scratch=[wide], aliases={0: 0})
    pay, n, v0 = call(first_row_kernel, [VEC, VEC, VEC], e, over_cols(pay), m, lt)
    (pay,) = call(col_kernel, [VEC], e, over_rows(pay), ls, v0, scratch=[wide])
    (pay,) = call(row_kernel, [VEC], e, over_cols(pay), lt, v0, scratch=[pltpu.VMEM(VEC, F32)])
    pay, f = call(
        last_kernel, [VEC, jax.ShapeDtypeStruct((H, L), F32)], place, e, over_rows(pay), ls, v0, alpha, sq, scratch=[wide, pltpu.VMEM(VEC, F32)]
    )
    total = jnp.sum(over_cols(pay), axis=0)
    g = -eps * ((jnp.log2(total) + n) / LOG2E - 2.0 * lt)
    g = lax.all_gather(g, "c").transpose(1, 0, 2).reshape(2 * N)
    return f.reshape(N // 2), g


def solution(mesh):
    grid = Mesh(mesh.devices.reshape(4, 4, 2, 8), ("x", "y", "c", "z"))
    src, tgt = ("x", "y", "c"), "z"
    in_specs = (P((*src, tgt), None), P((tgt, *src), None), P(src), P(tgt))
    return jax.shard_map(local, mesh=grid, in_specs=in_specs, out_specs=(P(src), P(tgt)), check_vma=False)
```

```python
import functools
import math

import jax
import jax.numpy as jnp
from jax import lax
from jax.experimental import pallas as pl
from jax.experimental.pallas import tpu as pltpu
from jax.sharding import Mesh
from jax.sharding import PartitionSpec as P

eps = 0.05
LOG2E = math.log2(math.e)
KAPPA = LOG2E / eps
SHIFT = 43.0
L = 128
B = 16
H = B // 2
N = B * L
F32 = jnp.float32
BF16 = jnp.bfloat16
VM = pl.BlockSpec(memory_space=pltpu.VMEM)
SM = pl.BlockSpec(memory_space=pltpu.SMEM)
VEC = (B, L)
NEAR = (0, 1, 7, 2, 6)
FAR = (3, 5, 4)
PARTS = ((0, 0), (0, 1), (1, 0), (1, 1), (0, 2), (2, 0))


def rows_of(q):
    return pl.ds(pl.multiple_of(q * L, L), L)


def lanes_of(s):
    return pl.ds(s * L, L)


def fold(x, op):
    return op(x.reshape(-1, 8, L), axis=0)


def spread(vec, out_ref):
    turned = jnp.concatenate([vec, jnp.zeros((L - B, L), F32)], axis=0).T
    for q in range(B):
        out_ref[q * L : (q + 1) * L, :] = jnp.broadcast_to(turned[:, q : q + 1], (L, L))


def split3(x):
    a = x.astype(BF16)
    x = x - a.astype(F32)
    b = x.astype(BF16)
    x = x - b.astype(F32)
    return a, b, x.astype(BF16)


def start_kernel(
    place_ref, near_ref, near_other_ref, far_ref, far_other_ref, tgt_ref, mass_ref, ls_other_ref,
    z_ref, pay_ref, sq_ref, ls_ref, s6, t6, beta,
):
    core, level = place_ref[0], place_ref[1]
    ls_ref[pl.ds(pl.multiple_of(core * H, H), H), :] = mass_ref[B:, :]
    ls_ref[pl.ds(pl.multiple_of((1 - core) * H, H), H), :] = ls_other_ref[...]
    for own, order, ref in (
        (True, NEAR, near_ref), (False, NEAR, near_other_ref), (True, FAR, far_ref), (False, FAR, far_other_ref),
    ):
        for at, step in enumerate(order):
            x = ref[at * L : (at + 1) * L, :]
            q = lax.rem(level + (H - step), H)
            if own:
                sq_ref[pl.ds(q, 1), :] = jnp.sum((x * x).T, axis=0, keepdims=True)
            parts = split3(x * (2.0 * KAPPA))
            rows = rows_of((core if own else 1 - core) * H + q)
            for c, (a, _) in enumerate(PARTS):
                s6[rows, c * L : (c + 1) * L] = parts[a]
    for q in range(B):
        t = tgt_ref[q * L : (q + 1) * L, :].T
        beta[q : q + 1, :] = LOG2E * mass_ref[q : q + 1, :] - KAPPA * jnp.sum(t * t, axis=0, keepdims=True)
        parts = split3(t)
        for c, (_, b) in enumerate(PARTS):
            t6[c * L : (c + 1) * L, q * L : (q + 1) * L] = parts[b]

    def product(rows, c):
        g = jnp.dot(s6[rows, :], t6[:, c * L : (c + 2) * L], preferred_element_type=F32)
        for s in range(2):
            z_ref[rows, lanes_of(c + s)] = g[:, s * L : (s + 1) * L] + beta[c + s : c + s + 1, :]

    def stats(q):
        rows = pl.ds(q * L, L)
        peak = z_ref[rows, lanes_of(0)]
        for s in range(1, B):
            peak = jnp.maximum(peak, z_ref[rows, lanes_of(s)])
        total = jnp.zeros((L, L), F32)
        for s in range(B):
            total = total + jnp.exp2(z_ref[rows, lanes_of(s)] - peak)
        peak = peak.T
        top = jnp.max(peak, axis=0, keepdims=True)
        pay_ref[q : q + 1, :] = top + jnp.log2(jnp.sum(total.T * jnp.exp2(peak - top), axis=0, keepdims=True))

    for half in range(3):
        for step in range(H):
            if half < 2:
                product(pl.ds(half * H * L, H * L), 2 * step)
            if half:
                stats((half - 1) * H + step)


def merge(got_ref):
    got = [got_ref[d] for d in range(B)]
    top = functools.reduce(jnp.maximum, got)
    return top + jnp.log2(functools.reduce(jnp.add, [jnp.exp2(x - top) for x in got]))


def add_up(got_ref):
    return functools.reduce(jnp.add, [got_ref[d] for d in range(B)])


def cols_kernel(z_ref, got_ref, ls_ref, e_ref, pay_ref, m_ref, alpha_ref, wide):
    alpha = LOG2E * ls_ref[...] - merge(got_ref)
    alpha_ref[...] = alpha
    spread(alpha, wide)

    def highest(q, peak):
        a = wide[rows_of(q), :]
        return tuple(jnp.maximum(peak[s], fold(z_ref[rows_of(q), lanes_of(s)] + a, jnp.max)) for s in range(B))

    peak = lax.fori_loop(0, B, highest, (jnp.full((8, L), -1e30, F32),) * B, unroll=2)
    for s in range(B):
        m_ref[s : s + 1, :] = jnp.max(peak[s], axis=0, keepdims=True)

    ahead = 3
    for c in range(0, B, H):

        def weigh(q, total, c=c):
            rows = pl.ds(pl.multiple_of(q * (L // 2), L // 2), L // 2)
            a = wide[rows, :] + SHIFT
            held = [z_ref[rows, lanes_of(c + s)] for s in range(ahead)]
            out = []
            for s in range(H):
                if s + ahead < H:
                    held.append(z_ref[rows, lanes_of(c + s + ahead)])
                e = jnp.exp2((held[s] + a) - m_ref[c + s : c + s + 1, :])
                e_ref[rows, lanes_of(c + s)] = e
                out.append(total[s] + fold(e, jnp.sum))
            return tuple(out)

        total = lax.fori_loop(0, 2 * B, weigh, (jnp.zeros((8, L), F32),) * H, unroll=2)
        for s in range(H):
            one = slice(c + s, c + s + 1)
            pay_ref[one, :] = m_ref[one, :] + (jnp.log2(jnp.sum(total[s], axis=0, keepdims=True)) - SHIFT)


def row_sums(e_ref, v_ref, pay_ref):
    def body(q, _):
        total = jnp.zeros((L, L), F32)
        for s in range(B):
            total = total + e_ref[rows_of(q), lanes_of(s)] * v_ref[s : s + 1, :]
        pay_ref[pl.ds(q, 1), :] = jnp.sum(total.T, axis=0, keepdims=True)
        return 0

    lax.fori_loop(0, B, body, 0, unroll=8)


def col_sums(e_ref, v0_ref, pay_ref, wide):
    def body(q, carry):
        u = wide[rows_of(q), :]
        return tuple(carry[s] + fold(e_ref[rows_of(q), lanes_of(s)] * u, jnp.sum) for s in range(B))

    done = lax.fori_loop(0, B, body, (jnp.zeros((8, L), F32),) * B, unroll=8)
    for s in range(B):
        pay_ref[s : s + 1, :] = v0_ref[s : s + 1, :] * jnp.sum(done[s], axis=0, keepdims=True)


def first_row_kernel(e_ref, got_ref, m_ref, lt_ref, pay_ref, n_ref, v0_ref):
    n = merge(got_ref)
    n_ref[...] = n
    v0_ref[...] = jnp.exp2(m_ref[...] - n + (LOG2E * lt_ref[...] + SHIFT))
    row_sums(e_ref, v0_ref, pay_ref)


def col_kernel(e_ref, got_ref, ls_ref, v0_ref, pay_ref, wide):
    spread(jnp.exp2(LOG2E * ls_ref[...]) / add_up(got_ref), wide)
    col_sums(e_ref, v0_ref, pay_ref, wide)


def row_kernel(e_ref, got_ref, lt_ref, v0_ref, pay_ref, v):
    v[...] = v0_ref[...] * (jnp.exp2(LOG2E * lt_ref[...]) / add_up(got_ref))
    row_sums(e_ref, v, pay_ref)


def last_kernel(place_ref, e_ref, got_ref, ls_ref, v0_ref, alpha_ref, sq_ref, pay_ref, f_ref, wide, total):
    total[...] = add_up(got_ref)
    own = pl.ds(pl.multiple_of(place_ref[0] * H, H), H)
    f_ref[...] = sq_ref[...] - (eps / LOG2E) * (jnp.log2(total[own, :]) - 2.0 * SHIFT - alpha_ref[own, :])
    spread(jnp.exp2(LOG2E * ls_ref[...]) / total[...], wide)
    col_sums(e_ref, v0_ref, pay_ref, wide)


def call(kernel, outs, *args, scratch=(), limit=8, aliases=None):
    return pl.pallas_call(
        kernel,
        out_shape=[pltpu.VMEM(x, F32) if isinstance(x, tuple) else x for x in outs],
        in_specs=[SM if x.dtype == jnp.int32 else VM for x in args],
        out_specs=[VM] * len(outs),
        scratch_shapes=scratch,
        input_output_aliases=aliases or {},
        compiler_params=pltpu.CompilerParams(vmem_limit_bytes=limit * 2**20),
        name=kernel.__name__,
    )(*args)


def share(x, axes):
    return lax.all_to_all(jnp.broadcast_to(x[None], (B,) + x.shape), axes, 0, 0, tiled=True)


def over_rows(x):
    return share(x, ("c", "z"))


def over_cols(x):
    return share(x, ("x", "y"))


def swap(x):
    return lax.ppermute(x, "c", [(0, 1), (1, 0)])


def climb(x, step):
    return lax.ppermute(x, "z", [(z, (z + step) % H) for z in range(H)])


def local(sources, targets, log_src_mass, log_tgt_mass):
    c = lax.axis_index("c")
    place = jnp.stack([c, lax.axis_index("z")])
    ls = log_src_mass.reshape(H, L)
    lt = lax.dynamic_index_in_dim(log_tgt_mass.reshape(B, 2, L), c, 1, keepdims=False)
    tgt = over_cols(targets).reshape(N, L)
    blocks = {0: sources, H: sources}
    for step in range(1, H // 2):
        blocks[step] = climb(blocks[step - 1], 1)
        blocks[H - step] = climb(blocks[H - step + 1], H - 1)
    blocks[H // 2] = climb(blocks[H // 2 - 1], 1)
    near = jnp.concatenate([blocks[step] for step in NEAR])
    far = jnp.concatenate([blocks[step] for step in FAR])
    wide = pltpu.VMEM((N, L), F32)
    bits = [pltpu.VMEM((N, 6 * L), BF16), pltpu.VMEM((6 * L, N), BF16), pltpu.VMEM(VEC, F32)]
    z, pay, sq, ls = call(
        start_kernel, [(N, N), VEC, (H, L), VEC], place, near, swap(near), far, swap(far), tgt, jnp.concatenate([lt, ls]), swap(ls),
        scratch=bits, limit=24,
    )
    e, pay, m, alpha = call(cols_kernel, [(N, N), VEC, VEC, VEC], z, over_rows(pay), ls, scratch=[wide], aliases={0: 0})
    pay, n, v0 = call(first_row_kernel, [VEC, VEC, VEC], e, over_cols(pay), m, lt)
    (pay,) = call(col_kernel, [VEC], e, over_rows(pay), ls, v0, scratch=[wide])
    (pay,) = call(row_kernel, [VEC], e, over_cols(pay), lt, v0, scratch=[pltpu.VMEM(VEC, F32)])
    pay, f = call(
        last_kernel, [VEC, jax.ShapeDtypeStruct((H, L), F32)], place, e, over_rows(pay), ls, v0, alpha, sq, scratch=[wide, pltpu.VMEM(VEC, F32)]
    )
    total = jnp.sum(over_cols(pay), axis=0)
    g = -eps * ((jnp.log2(total) + n) / LOG2E - 2.0 * lt)
    g = lax.all_gather(g, "c").transpose(1, 0, 2).reshape(2 * N)
    return f.reshape(N // 2), g


def solution(mesh):
    grid = Mesh(mesh.devices.reshape(4, 4, 2, 8), ("x", "y", "c", "z"))
    src, tgt = ("x", "y", "c"), "z"
    in_specs = (P((*src, tgt), None), P((tgt, *src), None), P(src), P(tgt))
    return jax.shard_map(local, mesh=grid, in_specs=in_specs, out_specs=(P(src), P(tgt)), check_vma=False)
```

```python
import functools
import math

import jax
import jax.numpy as jnp
from jax import lax
from jax.experimental import pallas as pl
from jax.experimental.pallas import tpu as pltpu
from jax.sharding import Mesh
from jax.sharding import PartitionSpec as P

eps = 0.05
LOG2E = math.log2(math.e)
KAPPA = LOG2E / eps
SHIFT = 43.0
L = 128
B = 16
H = B // 2
N = B * L
F32 = jnp.float32
BF16 = jnp.bfloat16
VM = pl.BlockSpec(memory_space=pltpu.VMEM)
SM = pl.BlockSpec(memory_space=pltpu.SMEM)
VEC = (B, L)
NEAR = (0, 1, 7, 2, 6)
FAR = (3, 5, 4)
PARTS = ((0, 0), (0, 1), (1, 0), (1, 1), (0, 2), (2, 0))


def rows_of(q):
    return pl.ds(pl.multiple_of(q * L, L), L)


def lanes_of(s):
    return pl.ds(s * L, L)


def fold(x, op):
    return op(x.reshape(-1, 8, L), axis=0)


def spread(vec, out_ref):
    turned = jnp.concatenate([vec, jnp.zeros((L - B, L), F32)], axis=0).T
    for q in range(B):
        out_ref[q * L : (q + 1) * L, :] = jnp.broadcast_to(turned[:, q : q + 1], (L, L))


def split3(x):
    a = x.astype(BF16)
    x = x - a.astype(F32)
    b = x.astype(BF16)
    x = x - b.astype(F32)
    return a, b, x.astype(BF16)


def start_kernel(
    place_ref, near_ref, near_other_ref, far_ref, far_other_ref, tgt_ref, mass_ref, ls_other_ref,
    z_ref, pay_ref, sq_ref, ls_ref, s6, t6, beta,
):
    core, level = place_ref[0], place_ref[1]
    ls_ref[pl.ds(pl.multiple_of(core * H, H), H), :] = mass_ref[B:, :]
    ls_ref[pl.ds(pl.multiple_of((1 - core) * H, H), H), :] = ls_other_ref[...]
    for own, order, ref in (
        (True, NEAR, near_ref), (False, NEAR, near_other_ref), (True, FAR, far_ref), (False, FAR, far_other_ref),
    ):
        for at, step in enumerate(order):
            x = ref[at * L : (at + 1) * L, :]
            q = lax.rem(level + (H - step), H)
            if own:
                sq_ref[pl.ds(q, 1), :] = jnp.sum((x * x).T, axis=0, keepdims=True)
            parts = split3(x * (2.0 * KAPPA))
            rows = rows_of((core if own else 1 - core) * H + q)
            for c, (a, _) in enumerate(PARTS):
                s6[rows, c * L : (c + 1) * L] = parts[a]
    for q in range(B):
        t = tgt_ref[q * L : (q + 1) * L, :].T
        beta[q : q + 1, :] = LOG2E * mass_ref[q : q + 1, :] - KAPPA * jnp.sum(t * t, axis=0, keepdims=True)
        parts = split3(t)
        for c, (_, b) in enumerate(PARTS):
            t6[c * L : (c + 1) * L, q * L : (q + 1) * L] = parts[b]

    def product(rows, c):
        g = jnp.dot(s6[rows, :], t6[:, c * L : (c + 2) * L], preferred_element_type=F32)
        for s in range(2):
            z_ref[rows, lanes_of(c + s)] = g[:, s * L : (s + 1) * L] + beta[c + s : c + s + 1, :]

    def stats(q):
        rows = pl.ds(q * L, L)
        peak = z_ref[rows, lanes_of(0)]
        for s in range(1, B):
            peak = jnp.maximum(peak, z_ref[rows, lanes_of(s)])
        total = jnp.zeros((L, L), F32)
        for s in range(B):
            total = total + jnp.exp2(z_ref[rows, lanes_of(s)] - peak)
        peak = peak.T
        top = jnp.max(peak, axis=0, keepdims=True)
        pay_ref[q : q + 1, :] = top + jnp.log2(jnp.sum(total.T * jnp.exp2(peak - top), axis=0, keepdims=True))

    for half in range(3):
        for step in range(H):
            if half < 2:
                product(pl.ds(half * H * L, H * L), 2 * step)
            if half:
                stats((half - 1) * H + step)


def merge(got_ref):
    got = [got_ref[d] for d in range(B)]
    top = functools.reduce(jnp.maximum, got)
    return top + jnp.log2(functools.reduce(jnp.add, [jnp.exp2(x - top) for x in got]))


def add_up(got_ref):
    return functools.reduce(jnp.add, [got_ref[d] for d in range(B)])


def cols_kernel(z_ref, got_ref, ls_ref, e_ref, pay_ref, m_ref, alpha_ref, wide):
    alpha = LOG2E * ls_ref[...] - merge(got_ref)
    alpha_ref[...] = alpha
    spread(alpha, wide)

    def highest(q, peak):
        a = wide[rows_of(q), :]
        return tuple(jnp.maximum(peak[s], fold(z_ref[rows_of(q), lanes_of(s)] + a, jnp.max)) for s in range(B))

    peak = lax.fori_loop(0, B, highest, (jnp.full((8, L), -1e30, F32),) * B, unroll=2)
    for s in range(B):
        m_ref[s : s + 1, :] = jnp.max(peak[s], axis=0, keepdims=True)

    ahead = 3
    for c in range(0, B, H):

        def weigh(q, total, c=c):
            rows = pl.ds(pl.multiple_of(q * (L // 2), L // 2), L // 2)
            a = wide[rows, :] + SHIFT
            held = [z_ref[rows, lanes_of(c + s)] for s in range(ahead)]
            out = []
            for s in range(H):
                if s + ahead < H:
                    held.append(z_ref[rows, lanes_of(c + s + ahead)])
                e = jnp.exp2((held[s] + a) - m_ref[c + s : c + s + 1, :])
                e_ref[rows, lanes_of(c + s)] = e
                out.append(total[s] + fold(e, jnp.sum))
            return tuple(out)

        total = lax.fori_loop(0, 2 * B, weigh, (jnp.zeros((8, L), F32),) * H, unroll=2)
        for s in range(H):
            one = slice(c + s, c + s + 1)
            pay_ref[one, :] = m_ref[one, :] + (jnp.log2(jnp.sum(total[s], axis=0, keepdims=True)) - SHIFT)


def row_sums(e_ref, v_ref, pay_ref):
    def body(q, _):
        total = jnp.zeros((L, L), F32)
        for s in range(B):
            total = total + e_ref[rows_of(q), lanes_of(s)] * v_ref[s : s + 1, :]
        pay_ref[pl.ds(q, 1), :] = jnp.sum(total.T, axis=0, keepdims=True)
        return 0

    lax.fori_loop(0, B, body, 0, unroll=8)


def col_sums(e_ref, v0_ref, pay_ref, wide):
    def body(q, carry):
        u = wide[rows_of(q), :]
        return tuple(carry[s] + fold(e_ref[rows_of(q), lanes_of(s)] * u, jnp.sum) for s in range(B))

    done = lax.fori_loop(0, B, body, (jnp.zeros((8, L), F32),) * B, unroll=8)
    for s in range(B):
        pay_ref[s : s + 1, :] = v0_ref[s : s + 1, :] * jnp.sum(done[s], axis=0, keepdims=True)


def first_row_kernel(e_ref, got_ref, m_ref, lt_ref, pay_ref, n_ref, v0_ref):
    n = merge(got_ref)
    n_ref[...] = n
    v0_ref[...] = jnp.exp2(m_ref[...] - n + (LOG2E * lt_ref[...] + SHIFT))
    row_sums(e_ref, v0_ref, pay_ref)


def col_kernel(e_ref, got_ref, ls_ref, v0_ref, pay_ref, wide):
    spread(jnp.exp2(LOG2E * ls_ref[...]) / add_up(got_ref), wide)
    col_sums(e_ref, v0_ref, pay_ref, wide)


def row_kernel(e_ref, got_ref, lt_ref, v0_ref, pay_ref, v):
    v[...] = v0_ref[...] * (jnp.exp2(LOG2E * lt_ref[...]) / add_up(got_ref))
    row_sums(e_ref, v, pay_ref)


def last_kernel(place_ref, e_ref, got_ref, ls_ref, v0_ref, alpha_ref, sq_ref, pay_ref, f_ref, wide, total):
    total[...] = add_up(got_ref)
    own = pl.ds(pl.multiple_of(place_ref[0] * H, H), H)
    f_ref[...] = sq_ref[...] - (eps / LOG2E) * (jnp.log2(total[own, :]) - 2.0 * SHIFT - alpha_ref[own, :])
    spread(jnp.exp2(LOG2E * ls_ref[...]) / total[...], wide)
    col_sums(e_ref, v0_ref, pay_ref, wide)


def call(kernel, outs, *args, scratch=(), limit=8, aliases=None):
    return pl.pallas_call(
        kernel,
        out_shape=[pltpu.VMEM(x, F32) if isinstance(x, tuple) else x for x in outs],
        in_specs=[SM if x.dtype == jnp.int32 else VM for x in args],
        out_specs=[VM] * len(outs),
        scratch_shapes=scratch,
        input_output_aliases=aliases or {},
        compiler_params=pltpu.CompilerParams(vmem_limit_bytes=limit * 2**20),
        name=kernel.__name__,
    )(*args)


def share(x, axes):
    return lax.all_to_all(jnp.broadcast_to(x[None], (B,) + x.shape), axes, 0, 0, tiled=True)


def over_rows(x):
    return share(x, ("c", "z"))


def over_cols(x):
    return share(x, ("x", "y"))


def swap(x):
    return lax.ppermute(x, "c", [(0, 1), (1, 0)])


def climb(x, step):
    return lax.ppermute(x, "z", [(z, (z + step) % H) for z in range(H)])


def local(sources, targets, log_src_mass, log_tgt_mass):
    c = lax.axis_index("c")
    place = jnp.stack([c, lax.axis_index("z")])
    ls = log_src_mass.reshape(H, L)
    lt = lax.dynamic_index_in_dim(log_tgt_mass.reshape(B, 2, L), c, 1, keepdims=False)
    tgt = over_cols(targets).reshape(N, L)
    blocks = {0: sources, H: sources}
    for step in range(1, H // 2):
        blocks[step] = climb(blocks[step - 1], 1)
        blocks[H - step] = climb(blocks[H - step + 1], H - 1)
    blocks[H // 2] = climb(blocks[H // 2 - 2], 2)
    near = jnp.concatenate([blocks[step] for step in NEAR])
    far = jnp.concatenate([blocks[step] for step in FAR])
    wide = pltpu.VMEM((N, L), F32)
    bits = [pltpu.VMEM((N, 6 * L), BF16), pltpu.VMEM((6 * L, N), BF16), pltpu.VMEM(VEC, F32)]
    z, pay, sq, ls = call(
        start_kernel, [(N, N), VEC, (H, L), VEC], place, near, swap(near), far, swap(far), tgt, jnp.concatenate([lt, ls]), swap(ls),
        scratch=bits, limit=24,
    )
    e, pay, m, alpha = call(cols_kernel, [(N, N), VEC, VEC, VEC], z, over_rows(pay), ls, scratch=[wide], aliases={0: 0})
    pay, n, v0 = call(first_row_kernel, [VEC, VEC, VEC], e, over_cols(pay), m, lt)
    (pay,) = call(col_kernel, [VEC], e, over_rows(pay), ls, v0, scratch=[wide])
    (pay,) = call(row_kernel, [VEC], e, over_cols(pay), lt, v0, scratch=[pltpu.VMEM(VEC, F32)])
    pay, f = call(
        last_kernel, [VEC, jax.ShapeDtypeStruct((H, L), F32)], place, e, over_rows(pay), ls, v0, alpha, sq, scratch=[wide, pltpu.VMEM(VEC, F32)]
    )
    total = jnp.sum(over_cols(pay), axis=0)
    g = -eps * ((jnp.log2(total) + n) / LOG2E - 2.0 * lt)
    g = lax.all_gather(g, "c").transpose(1, 0, 2).reshape(2 * N)
    return f.reshape(N // 2), g


def solution(mesh):
    grid = Mesh(mesh.devices.reshape(4, 4, 2, 8), ("x", "y", "c", "z"))
    src, tgt = ("x", "y", "c"), "z"
    in_specs = (P((*src, tgt), None), P((tgt, *src), None), P(src), P(tgt))
    return jax.shard_map(local, mesh=grid, in_specs=in_specs, out_specs=(P(src), P(tgt)), check_vma=False)
```

```python
import functools
import math

import jax
import jax.numpy as jnp
from jax import lax
from jax.experimental import pallas as pl
from jax.experimental.pallas import tpu as pltpu
from jax.sharding import Mesh
from jax.sharding import PartitionSpec as P

eps = 0.05
LOG2E = math.log2(math.e)
KAPPA = LOG2E / eps
SHIFT = 43.0
L = 128
B = 16
H = B // 2
N = B * L
F32 = jnp.float32
BF16 = jnp.bfloat16
VM = pl.BlockSpec(memory_space=pltpu.VMEM)
SM = pl.BlockSpec(memory_space=pltpu.SMEM)
VEC = (B, L)
NEAR = (0, 1, 7, 2, 6)
FAR = (3, 5, 4)
PARTS = ((0, 0), (0, 1), (1, 0), (1, 1), (0, 2), (2, 0))


def rows_of(q):
    return pl.ds(pl.multiple_of(q * L, L), L)


def lanes_of(s):
    return pl.ds(s * L, L)


def fold(x, op):
    return op(x.reshape(-1, 8, L), axis=0)


def spread(vec, out_ref):
    turned = jnp.concatenate([vec, jnp.zeros((L - B, L), F32)], axis=0).T
    for q in range(B):
        out_ref[q * L : (q + 1) * L, :] = jnp.broadcast_to(turned[:, q : q + 1], (L, L))


def split3(x):
    a = x.astype(BF16)
    x = x - a.astype(F32)
    b = x.astype(BF16)
    x = x - b.astype(F32)
    return a, b, x.astype(BF16)


def fan_kernel(x_ref, out_ref):
    for d in range(B):
        out_ref[d] = x_ref[...]


def start_kernel(
    place_ref, near_ref, near_other_ref, far_ref, far_other_ref, tgt_ref, mass_ref, ls_other_ref,
    z_ref, pay_ref, sq_ref, ls_ref, s6, t6, beta,
):
    core, level = place_ref[0], place_ref[1]
    ls_ref[pl.ds(pl.multiple_of(core * H, H), H), :] = mass_ref[B:, :]
    ls_ref[pl.ds(pl.multiple_of((1 - core) * H, H), H), :] = ls_other_ref[...]
    for own, order, ref in (
        (True, NEAR, near_ref), (False, NEAR, near_other_ref), (True, FAR, far_ref), (False, FAR, far_other_ref),
    ):
        for at, step in enumerate(order):
            x = ref[at * L : (at + 1) * L, :]
            q = lax.rem(level + (H - step), H)
            if own:
                sq_ref[pl.ds(q, 1), :] = jnp.sum((x * x).T, axis=0, keepdims=True)
            parts = split3(x * (2.0 * KAPPA))
            rows = rows_of((core if own else 1 - core) * H + q)
            for c, (a, _) in enumerate(PARTS):
                s6[rows, c * L : (c + 1) * L] = parts[a]
    for q in range(B):
        t = tgt_ref[q * L : (q + 1) * L, :].T
        beta[q : q + 1, :] = LOG2E * mass_ref[q : q + 1, :] - KAPPA * jnp.sum(t * t, axis=0, keepdims=True)
        parts = split3(t)
        for c, (_, b) in enumerate(PARTS):
            t6[c * L : (c + 1) * L, q * L : (q + 1) * L] = parts[b]

    def product(rows, c):
        g = jnp.dot(s6[rows, :], t6[:, c * L : (c + 2) * L], preferred_element_type=F32)
        for s in range(2):
            z_ref[rows, lanes_of(c + s)] = g[:, s * L : (s + 1) * L] + beta[c + s : c + s + 1, :]

    def stats(q):
        rows = pl.ds(q * L, L)
        peak = z_ref[rows, lanes_of(0)]
        for s in range(1, B):
            peak = jnp.maximum(peak, z_ref[rows, lanes_of(s)])
        total = jnp.zeros((L, L), F32)
        for s in range(B):
            total = total + jnp.exp2(z_ref[rows, lanes_of(s)] - peak)
        peak = peak.T
        top = jnp.max(peak, axis=0, keepdims=True)
        pay_ref[q : q + 1, :] = top + jnp.log2(jnp.sum(total.T * jnp.exp2(peak - top), axis=0, keepdims=True))

    for half in range(3):
        for step in range(H):
            if half < 2:
                product(pl.ds(half * H * L, H * L), 2 * step)
            if half:
                stats((half - 1) * H + step)


def merge(got_ref):
    got = [got_ref[d] for d in range(B)]
    top = functools.reduce(jnp.maximum, got)
    return top + jnp.log2(functools.reduce(jnp.add, [jnp.exp2(x - top) for x in got]))


def add_up(got_ref):
    return functools.reduce(jnp.add, [got_ref[d] for d in range(B)])


def cols_kernel(z_ref, got_ref, ls_ref, e_ref, pay_ref, m_ref, alpha_ref, wide):
    alpha = LOG2E * ls_ref[...] - merge(got_ref)
    alpha_ref[...] = alpha
    spread(alpha, wide)

    def highest(q, peak):
        a = wide[rows_of(q), :]
        return tuple(jnp.maximum(peak[s], fold(z_ref[rows_of(q), lanes_of(s)] + a, jnp.max)) for s in range(B))

    peak = lax.fori_loop(0, B, highest, (jnp.full((8, L), -1e30, F32),) * B, unroll=2)
    for s in range(B):
        m_ref[s : s + 1, :] = jnp.max(peak[s], axis=0, keepdims=True)

    ahead = 3
    for c in range(0, B, H):

        def weigh(q, total, c=c):
            rows = pl.ds(pl.multiple_of(q * (L // 2), L // 2), L // 2)
            a = wide[rows, :] + SHIFT
            held = [z_ref[rows, lanes_of(c + s)] for s in range(ahead)]
            out = []
            for s in range(H):
                if s + ahead < H:
                    held.append(z_ref[rows, lanes_of(c + s + ahead)])
                e = jnp.exp2((held[s] + a) - m_ref[c + s : c + s + 1, :])
                e_ref[rows, lanes_of(c + s)] = e
                out.append(total[s] + fold(e, jnp.sum))
            return tuple(out)

        total = lax.fori_loop(0, 2 * B, weigh, (jnp.zeros((8, L), F32),) * H, unroll=2)
        for s in range(H):
            one = slice(c + s, c + s + 1)
            pay_ref[one, :] = m_ref[one, :] + (jnp.log2(jnp.sum(total[s], axis=0, keepdims=True)) - SHIFT)


def row_sums(e_ref, v_ref, pay_ref):
    def body(q, _):
        total = jnp.zeros((L, L), F32)
        for s in range(B):
            total = total + e_ref[rows_of(q), lanes_of(s)] * v_ref[s : s + 1, :]
        pay_ref[pl.ds(q, 1), :] = jnp.sum(total.T, axis=0, keepdims=True)
        return 0

    lax.fori_loop(0, B, body, 0, unroll=8)


def col_sums(e_ref, v0_ref, pay_ref, wide):
    def body(q, carry):
        u = wide[rows_of(q), :]
        return tuple(carry[s] + fold(e_ref[rows_of(q), lanes_of(s)] * u, jnp.sum) for s in range(B))

    done = lax.fori_loop(0, B, body, (jnp.zeros((8, L), F32),) * B, unroll=8)
    for s in range(B):
        pay_ref[s : s + 1, :] = v0_ref[s : s + 1, :] * jnp.sum(done[s], axis=0, keepdims=True)


def first_row_kernel(e_ref, got_ref, m_ref, lt_ref, pay_ref, n_ref, v0_ref):
    n = merge(got_ref)
    n_ref[...] = n
    v0_ref[...] = jnp.exp2(m_ref[...] - n + (LOG2E * lt_ref[...] + SHIFT))
    row_sums(e_ref, v0_ref, pay_ref)


def col_kernel(e_ref, got_ref, ls_ref, v0_ref, pay_ref, wide):
    spread(jnp.exp2(LOG2E * ls_ref[...]) / add_up(got_ref), wide)
    col_sums(e_ref, v0_ref, pay_ref, wide)


def row_kernel(e_ref, got_ref, lt_ref, v0_ref, pay_ref, v):
    v[...] = v0_ref[...] * (jnp.exp2(LOG2E * lt_ref[...]) / add_up(got_ref))
    row_sums(e_ref, v, pay_ref)


def last_kernel(place_ref, e_ref, got_ref, ls_ref, v0_ref, alpha_ref, sq_ref, pay_ref, f_ref, wide, total):
    total[...] = add_up(got_ref)
    own = pl.ds(pl.multiple_of(place_ref[0] * H, H), H)
    f_ref[...] = sq_ref[...] - (eps / LOG2E) * (jnp.log2(total[own, :]) - 2.0 * SHIFT - alpha_ref[own, :])
    spread(jnp.exp2(LOG2E * ls_ref[...]) / total[...], wide)
    col_sums(e_ref, v0_ref, pay_ref, wide)


def call(kernel, outs, *args, scratch=(), limit=8, aliases=None):
    return pl.pallas_call(
        kernel,
        out_shape=[pltpu.VMEM(x, F32) if isinstance(x, tuple) else x for x in outs],
        in_specs=[SM if x.dtype == jnp.int32 else VM for x in args],
        out_specs=[VM] * len(outs),
        scratch_shapes=scratch,
        input_output_aliases=aliases or {},
        compiler_params=pltpu.CompilerParams(vmem_limit_bytes=limit * 2**20),
        name=kernel.__name__,
    )(*args)


def share(x, axes):
    return lax.all_to_all(jnp.broadcast_to(x[None], (B,) + x.shape), axes, 0, 0, tiled=True)


def over_rows(x):
    return share(x, ("c", "z"))


def over_cols(x):
    return share(x, ("x", "y"))


def swap(x):
    return lax.ppermute(x, "c", [(0, 1), (1, 0)])


def climb(x, step):
    return lax.ppermute(x, "z", [(z, (z + step) % H) for z in range(H)])


def local(sources, targets, log_src_mass, log_tgt_mass):
    c = lax.axis_index("c")
    place = jnp.stack([c, lax.axis_index("z")])
    ls = log_src_mass.reshape(H, L)
    lt = lax.dynamic_index_in_dim(log_tgt_mass.reshape(B, 2, L), c, 1, keepdims=False)
    (fan,) = call(fan_kernel, [jax.ShapeDtypeStruct((B, L, L), F32)], targets)
    tgt = lax.all_to_all(fan, ("x", "y"), 0, 0, tiled=True).reshape(N, L)
    blocks = {0: sources, H: sources}
    for step in range(1, H // 2):
        blocks[step] = climb(blocks[step - 1], 1)
        blocks[H - step] = climb(blocks[H - step + 1], H - 1)
    blocks[H // 2] = climb(blocks[H // 2 - 2], 2)
    mass, blocks[H // 2] = lax.optimization_barrier((jnp.concatenate([lt, ls]), blocks[H // 2]))
    near = jnp.concatenate([blocks[step] for step in NEAR])
    far = jnp.concatenate([blocks[step] for step in FAR])
    wide = pltpu.VMEM((N, L), F32)
    bits = [pltpu.VMEM((N, 6 * L), BF16), pltpu.VMEM((6 * L, N), BF16), pltpu.VMEM(VEC, F32)]
    z, pay, sq, ls = call(
        start_kernel, [(N, N), VEC, (H, L), VEC], place, near, swap(near), far, swap(far), tgt, mass, swap(ls),
        scratch=bits, limit=24,
    )
    e, pay, m, alpha = call(cols_kernel, [(N, N), VEC, VEC, VEC], z, over_rows(pay), ls, scratch=[wide], aliases={0: 0})
    pay, n, v0 = call(first_row_kernel, [VEC, VEC, VEC], e, over_cols(pay), m, lt)
    (pay,) = call(col_kernel, [VEC], e, over_rows(pay), ls, v0, scratch=[wide])
    (pay,) = call(row_kernel, [VEC], e, over_cols(pay), lt, v0, scratch=[pltpu.VMEM(VEC, F32)])
    pay, f = call(
        last_kernel, [VEC, jax.ShapeDtypeStruct((H, L), F32)], place, e, over_rows(pay), ls, v0, alpha, sq, scratch=[wide, pltpu.VMEM(VEC, F32)]
    )
    total = jnp.sum(over_cols(pay), axis=0)
    g = -eps * ((jnp.log2(total) + n) / LOG2E - 2.0 * lt)
    g = lax.all_gather(g, "c").transpose(1, 0, 2).reshape(2 * N)
    return f.reshape(N // 2), g


def solution(mesh):
    grid = Mesh(mesh.devices.reshape(4, 4, 2, 8), ("x", "y", "c", "z"))
    src, tgt = ("x", "y", "c"), "z"
    in_specs = (P((*src, tgt), None), P((tgt, *src), None), P(src), P(tgt))
    return jax.shard_map(local, mesh=grid, in_specs=in_specs, out_specs=(P(src), P(tgt)), check_vma=False)
```

```python
import functools
import math

import jax
import jax.numpy as jnp
from jax import lax
from jax.experimental import pallas as pl
from jax.experimental.pallas import tpu as pltpu
from jax.sharding import Mesh
from jax.sharding import PartitionSpec as P

eps = 0.05
LOG2E = math.log2(math.e)
KAPPA = LOG2E / eps
SHIFT = 43.0
L = 128
B = 16
H = B // 2
N = B * L
F32 = jnp.float32
BF16 = jnp.bfloat16
VM = pl.BlockSpec(memory_space=pltpu.VMEM)
SM = pl.BlockSpec(memory_space=pltpu.SMEM)
VEC = (B, L)
NEAR = (1, 7, 2, 6)
FAR = (0, 3, 5, 4)
PARTS = ((0, 0), (0, 1), (1, 0), (1, 1), (0, 2), (2, 0))


def rows_of(q):
    return pl.ds(pl.multiple_of(q * L, L), L)


def lanes_of(s):
    return pl.ds(s * L, L)


def fold(x, op):
    return op(x.reshape(-1, 8, L), axis=0)


def spread(vec, out_ref):
    turned = jnp.concatenate([vec, jnp.zeros((L - B, L), F32)], axis=0).T
    for q in range(B):
        out_ref[q * L : (q + 1) * L, :] = jnp.broadcast_to(turned[:, q : q + 1], (L, L))


def split3(x):
    a = x.astype(BF16)
    x = x - a.astype(F32)
    b = x.astype(BF16)
    x = x - b.astype(F32)
    return a, b, x.astype(BF16)


def start_kernel(
    place_ref, near_ref, near_other_ref, far_ref, far_other_ref, tgt_ref, mass_ref, ls_other_ref,
    z_ref, pay_ref, sq_ref, ls_ref, s6, t6, beta,
):
    core, level = place_ref[0], place_ref[1]
    ls_ref[pl.ds(pl.multiple_of(core * H, H), H), :] = mass_ref[B:, :]
    ls_ref[pl.ds(pl.multiple_of((1 - core) * H, H), H), :] = ls_other_ref[...]
    for own, order, ref in (
        (True, NEAR, near_ref), (False, NEAR, near_other_ref), (True, FAR, far_ref), (False, FAR, far_other_ref),
    ):
        for at, step in enumerate(order):
            x = ref[at * L : (at + 1) * L, :]
            q = lax.rem(level + (H - step), H)
            if own:
                sq_ref[pl.ds(q, 1), :] = jnp.sum((x * x).T, axis=0, keepdims=True)
            parts = split3(x * (2.0 * KAPPA))
            rows = rows_of((core if own else 1 - core) * H + q)
            for c, (a, _) in enumerate(PARTS):
                s6[rows, c * L : (c + 1) * L] = parts[a]
    for q in range(B):
        t = tgt_ref[q * L : (q + 1) * L, :].T
        beta[q : q + 1, :] = LOG2E * mass_ref[q : q + 1, :] - KAPPA * jnp.sum(t * t, axis=0, keepdims=True)
        parts = split3(t)
        for c, (_, b) in enumerate(PARTS):
            t6[c * L : (c + 1) * L, q * L : (q + 1) * L] = parts[b]

    def product(rows, c):
        g = jnp.dot(s6[rows, :], t6[:, c * L : (c + 2) * L], preferred_element_type=F32)
        for s in range(2):
            z_ref[rows, lanes_of(c + s)] = g[:, s * L : (s + 1) * L] + beta[c + s : c + s + 1, :]

    def stats(q):
        rows = pl.ds(q * L, L)
        peak = z_ref[rows, lanes_of(0)]
        for s in range(1, B):
            peak = jnp.maximum(peak, z_ref[rows, lanes_of(s)])
        total = jnp.zeros((L, L), F32)
        for s in range(B):
            total = total + jnp.exp2(z_ref[rows, lanes_of(s)] - peak)
        peak = peak.T
        top = jnp.max(peak, axis=0, keepdims=True)
        pay_ref[q : q + 1, :] = top + jnp.log2(jnp.sum(total.T * jnp.exp2(peak - top), axis=0, keepdims=True))

    for half in range(3):
        for step in range(H):
            if half < 2:
                product(pl.ds(half * H * L, H * L), 2 * step)
            if half:
                stats((half - 1) * H + step)


def merge(got_ref):
    got = [got_ref[d] for d in range(B)]
    top = functools.reduce(jnp.maximum, got)
    return top + jnp.log2(functools.reduce(jnp.add, [jnp.exp2(x - top) for x in got]))


def add_up(got_ref):
    return functools.reduce(jnp.add, [got_ref[d] for d in range(B)])


def cols_kernel(z_ref, got_ref, ls_ref, e_ref, pay_ref, m_ref, alpha_ref, wide):
    alpha = LOG2E * ls_ref[...] - merge(got_ref)
    alpha_ref[...] = alpha
    spread(alpha, wide)

    def highest(q, peak):
        a = wide[rows_of(q), :]
        return tuple(jnp.maximum(peak[s], fold(z_ref[rows_of(q), lanes_of(s)] + a, jnp.max)) for s in range(B))

    peak = lax.fori_loop(0, B, highest, (jnp.full((8, L), -1e30, F32),) * B, unroll=2)
    for s in range(B):
        m_ref[s : s + 1, :] = jnp.max(peak[s], axis=0, keepdims=True)

    ahead = 3
    for c in range(0, B, H):

        def weigh(q, total, c=c):
            rows = pl.ds(pl.multiple_of(q * (L // 2), L // 2), L // 2)
            a = wide[rows, :] + SHIFT
            held = [z_ref[rows, lanes_of(c + s)] for s in range(ahead)]
            out = []
            for s in range(H):
                if s + ahead < H:
                    held.append(z_ref[rows, lanes_of(c + s + ahead)])
                e = jnp.exp2((held[s] + a) - m_ref[c + s : c + s + 1, :])
                e_ref[rows, lanes_of(c + s)] = e
                out.append(total[s] + fold(e, jnp.sum))
            return tuple(out)

        total = lax.fori_loop(0, 2 * B, weigh, (jnp.zeros((8, L), F32),) * H, unroll=2)
        for s in range(H):
            one = slice(c + s, c + s + 1)
            pay_ref[one, :] = m_ref[one, :] + (jnp.log2(jnp.sum(total[s], axis=0, keepdims=True)) - SHIFT)


def row_sums(e_ref, v_ref, pay_ref):
    def body(q, _):
        total = jnp.zeros((L, L), F32)
        for s in range(B):
            total = total + e_ref[rows_of(q), lanes_of(s)] * v_ref[s : s + 1, :]
        pay_ref[pl.ds(q, 1), :] = jnp.sum(total.T, axis=0, keepdims=True)
        return 0

    lax.fori_loop(0, B, body, 0, unroll=8)


def col_sums(e_ref, v0_ref, pay_ref, wide):
    def body(q, carry):
        u = wide[rows_of(q), :]
        return tuple(carry[s] + fold(e_ref[rows_of(q), lanes_of(s)] * u, jnp.sum) for s in range(B))

    done = lax.fori_loop(0, B, body, (jnp.zeros((8, L), F32),) * B, unroll=8)
    for s in range(B):
        pay_ref[s : s + 1, :] = v0_ref[s : s + 1, :] * jnp.sum(done[s], axis=0, keepdims=True)


def first_row_kernel(e_ref, got_ref, m_ref, lt_ref, pay_ref, n_ref, v0_ref):
    n = merge(got_ref)
    n_ref[...] = n
    v0_ref[...] = jnp.exp2(m_ref[...] - n + (LOG2E * lt_ref[...] + SHIFT))
    row_sums(e_ref, v0_ref, pay_ref)


def col_kernel(e_ref, got_ref, ls_ref, v0_ref, pay_ref, wide):
    spread(jnp.exp2(LOG2E * ls_ref[...]) / add_up(got_ref), wide)
    col_sums(e_ref, v0_ref, pay_ref, wide)


def row_kernel(e_ref, got_ref, lt_ref, v0_ref, pay_ref, v):
    v[...] = v0_ref[...] * (jnp.exp2(LOG2E * lt_ref[...]) / add_up(got_ref))
    row_sums(e_ref, v, pay_ref)


def last_kernel(place_ref, e_ref, got_ref, ls_ref, v0_ref, alpha_ref, sq_ref, pay_ref, f_ref, wide, total):
    total[...] = add_up(got_ref)
    own = pl.ds(pl.multiple_of(place_ref[0] * H, H), H)
    f_ref[...] = sq_ref[...] - (eps / LOG2E) * (jnp.log2(total[own, :]) - 2.0 * SHIFT - alpha_ref[own, :])
    spread(jnp.exp2(LOG2E * ls_ref[...]) / total[...], wide)
    col_sums(e_ref, v0_ref, pay_ref, wide)


def call(kernel, outs, *args, scratch=(), limit=8, aliases=None):
    return pl.pallas_call(
        kernel,
        out_shape=[pltpu.VMEM(x, F32) if isinstance(x, tuple) else x for x in outs],
        in_specs=[SM if x.dtype == jnp.int32 else VM for x in args],
        out_specs=[VM] * len(outs),
        scratch_shapes=scratch,
        input_output_aliases=aliases or {},
        compiler_params=pltpu.CompilerParams(vmem_limit_bytes=limit * 2**20),
        name=kernel.__name__,
    )(*args)


def share(x, axes):
    return lax.all_to_all(jnp.broadcast_to(x[None], (B,) + x.shape), axes, 0, 0, tiled=True)


def over_rows(x):
    return share(x, ("c", "z"))


def over_cols(x):
    return share(x, ("x", "y"))


def swap(x):
    return lax.ppermute(x, "c", [(0, 1), (1, 0)])


def climb(x, step):
    return lax.ppermute(x, "z", [(z, (z + step) % H) for z in range(H)])


def local(sources, targets, log_src_mass, log_tgt_mass):
    c = lax.axis_index("c")
    place = jnp.stack([c, lax.axis_index("z")])
    ls = log_src_mass.reshape(H, L)
    lt = lax.dynamic_index_in_dim(log_tgt_mass.reshape(B, 2, L), c, 1, keepdims=False)
    tgt = over_cols(targets).reshape(N, L)
    blocks = {0: sources, H: sources}
    for step in range(1, H // 2):
        blocks[step] = climb(blocks[step - 1], 1)
        blocks[H - step] = climb(blocks[H - step + 1], H - 1)
    blocks[H // 2] = climb(blocks[H // 2 - 2], 2)
    blocks[0], blocks[2] = lax.optimization_barrier((sources, blocks[2]))
    near = jnp.concatenate([blocks[step] for step in NEAR])
    far = jnp.concatenate([blocks[step] for step in FAR])
    wide = pltpu.VMEM((N, L), F32)
    bits = [pltpu.VMEM((N, 6 * L), BF16), pltpu.VMEM((6 * L, N), BF16), pltpu.VMEM(VEC, F32)]
    z, pay, sq, ls = call(
        start_kernel, [(N, N), VEC, (H, L), VEC], place, near, swap(near), far, swap(far), tgt, jnp.concatenate([lt, ls]), swap(ls),
        scratch=bits, limit=24,
    )
    e, pay, m, alpha = call(cols_kernel, [(N, N), VEC, VEC, VEC], z, over_rows(pay), ls, scratch=[wide], aliases={0: 0})
    pay, n, v0 = call(first_row_kernel, [VEC, VEC, VEC], e, over_cols(pay), m, lt)
    (pay,) = call(col_kernel, [VEC], e, over_rows(pay), ls, v0, scratch=[wide])
    (pay,) = call(row_kernel, [VEC], e, over_cols(pay), lt, v0, scratch=[pltpu.VMEM(VEC, F32)])
    pay, f = call(
        last_kernel, [VEC, jax.ShapeDtypeStruct((H, L), F32)], place, e, over_rows(pay), ls, v0, alpha, sq, scratch=[wide, pltpu.VMEM(VEC, F32)]
    )
    total = jnp.sum(over_cols(pay), axis=0)
    g = -eps * ((jnp.log2(total) + n) / LOG2E - 2.0 * lt)
    g = lax.all_gather(g, "c").transpose(1, 0, 2).reshape(2 * N)
    return f.reshape(N // 2), g


def solution(mesh):
    grid = Mesh(mesh.devices.reshape(4, 4, 2, 8), ("x", "y", "c", "z"))
    src, tgt = ("x", "y", "c"), "z"
    in_specs = (P((*src, tgt), None), P((tgt, *src), None), P(src), P(tgt))
    return jax.shard_map(local, mesh=grid, in_specs=in_specs, out_specs=(P(src), P(tgt)), check_vma=False)
```
